32 devices in a mesh: group: 2 (over y), sec: 4 (over z), sub: 4 (over x, core).
Axes of the slice: x: 2, y: 2, z: 4, core: 2. Of those that a mesh axis runs over, the one named last changes fastest.
Arguments:
- tokens: bfloat16 [768, 2048], P(('group', 'sec'), 'sub'), parts along dimension 0, may hold values from -6 to 6
- routes: int32 [768, 2], P(('group', 'sec')), parts along dimension 0, may hold values from 0 to 3, all different within a row; in each aligned block of 96 rows (0 to 95, 96 to 191, ...) at most 96 rows name the same one
- router_weight: bfloat16 [2048, 4], replicated, may hold values from -0.25 to 0.25
- gate_weight: bfloat16 [4, 2048, 1536], P('sec', None, 'sub'), may hold values from -0.125 to 0.125
- up_weight: bfloat16 [4, 2048, 1536], P('sec', None, 'sub'), may hold values from -0.125 to 0.125
- down_weight: bfloat16 [4, 1536, 2048], P('sec', 'sub'), may hold values from -0.15625 to 0.15625
Outputs:
- mixed: bfloat16 [768, 2048], P(('group', 'sec'), 'sub'), parts along dimension 0
The draws below stay inside these ranges and needn't reach their ends.
There are 2 independent parts, one for each index of `group`. The reference program is written for one: setup_inputs(seed, part) draws one part's arguments, and reference() takes and returns one part's arrays. A program takes and returns all parts, laid end to end along the dimension named above; an argument that names none is the same for every part. Nothing has to cross between parts.
Inputs may be any that keep to these rules, and one draw needn't show every extreme that they name: `routes`: A row names 2 different experts. In each aligned block of 96 rows no expert is named more than 96 times, a bound that some block reaches.
All inputs are finite; a program needn't handle non-finite values.
Results may differ from the reference program's by a relative error of at most 0.012.
Values may be sent and summed in bfloat16 or wider, within the bound.
A program may use at most 64 MiB of HBM per device.

```python
import math
import jax
import jax.numpy as jnp
import numpy as np
from jax import lax

D = 2048
FF = 1536
ROWS_DEV = 96
EXPERTS = 4
TOP = 2
CAP = 96
HSHARD = 384
ROWS = 384
N_SEC = 4
N_SUB = 4


def level_of(rng, dims, shards, smallest, high):
    gain = 1.0
    for dim, blocks in shards:
        draws = jax.random.uniform(jax.random.fold_in(jax.random.fold_in(rng, 6), dim), (blocks,), jnp.float32, smallest / len(shards), high / len(shards))
        gain = gain * jnp.repeat(jnp.exp(draws), dims[dim] // blocks).reshape((-1,) + (1,) * (len(dims) - 1 - dim))
    return gain


def assign_block(own_key, own, number, rows, count, top, reach, lean):
    order = jax.random.permutation(own_key, count)
    crowded, ordinary = portions_of(count, rows * top, reach, lean, True), portions_of(count, rows * top, reach, lean, False)
    places = jnp.arange(count)

    def named(tallies, rotation):
        used = int((tallies > 0).sum())
        fixed = max(1, used // 4)
        moved = fixed + (places - fixed + rotation * (used - fixed)) % max(1, count - fixed)
        return jnp.zeros((count,), jnp.int32).at[order[jnp.where(places < fixed, places, moved)]].set(jnp.asarray(tallies, jnp.int32))

    tallies = jnp.where(number % 4 == 0, named(crowded, number // 4), named(ordinary, number - number // 4 - 1))
    mixed = jax.random.permutation(jax.random.fold_in(own, 3), count)
    giver, taker = mixed[0:count // 2 * 2:2], mixed[1:count // 2 * 2:2]
    slack = jnp.minimum(tallies[giver] - 1, reach - tallies[taker]) // 2
    slack = jnp.where((giver == order[0]) | (taker == order[0]) | (tallies[taker] == 0), 0, jnp.maximum(slack, 0))
    moved = jax.random.randint(jax.random.fold_in(own, 4), (count // 2,), 0, 1 << 20) % (slack + 1)
    tallies = tallies.at[giver].add(-moved).at[taker].add(moved)
    members = jnp.searchsorted(jnp.cumsum(tallies), jnp.arange(rows * top), side="right").astype(jnp.int32)
    listing = members.reshape(top, rows).T
    listing = listing[jax.random.permutation(jax.random.fold_in(own, 1), rows)]
    rotation = jax.random.randint(jax.random.fold_in(own, 2), (rows, 1), 0, top)
    return jnp.take_along_axis(listing, (jnp.arange(top)[None, :] + rotation) % top, axis=1)


def portions_of(count, total, bound, slope, full):
    weights = [(1 << 20) // math.isqrt(grade ** slope) + 1 for grade in range(1, count + 1)]
    largest = bound if full else min(bound, max(-(-total // count), total * weights[0] // sum(weights)))
    least = 1 if total - largest >= count - 1 else 0
    holding, spare = [largest] + [least] * (count - 1), total - largest - least * (count - 1)
    while spare > 0:
        candidates = [i for i in range(1, count) if holding[i] < largest] or [i for i in range(1, count) if holding[i] < bound]
        whole, remaining = sum([weights[i] for i in candidates]), spare
        for i in candidates:
            addition = min(bound - holding[i], max(1, remaining * weights[i] // whole), spare)
            holding[i] = holding[i] + addition
            spare = spare - addition
    return np.array(holding)


def bell_draw(own_key, dims, scale, most, pieces=(), kind=jnp.bfloat16):
    factor_of = level_of(own_key, dims, pieces, -0.22, 0.18) if pieces else 1.0
    entries = jax.random.normal(own_key, dims, jnp.float32) * scale * factor_of
    return jnp.minimum(jnp.maximum(entries, -most), most).astype(kind)


def setup_inputs(seed: int = 0, part: int = 0) -> dict:
    splits = jax.random.split(jax.random.key(seed), 7)
    part_keys = jax.random.split(jax.random.fold_in(splits[6], part), 7)
    tokens = bell_draw(part_keys[0], (ROWS, D), 1.0, 6.0, ((0, 4), (1, 4)))
    routes_keys = jax.random.split(jax.random.fold_in(part_keys[1], 1), ROWS // ROWS_DEV)
    routes_turns = jax.random.permutation(jax.random.fold_in(part_keys[1], 3), ROWS // ROWS_DEV)
    routes = jax.vmap(lambda own, number: assign_block(jax.random.fold_in(part_keys[1], 2), own, number, ROWS_DEV, EXPERTS, TOP, CAP, 2))(routes_keys, routes_turns).reshape((ROWS, TOP))
    router_weight = bell_draw(splits[2], (D, EXPERTS), (D // 4) ** -0.5, 0.25)
    gate_weight = bell_draw(splits[3], (EXPERTS, D, FF), D ** -0.5, 0.125, ((0, 4), (2, 4)))
    up_weight = bell_draw(splits[4], (EXPERTS, D, FF), D ** -0.5, 0.125, ((0, 4), (2, 4)))
    down_weight = bell_draw(splits[5], (EXPERTS, FF, D), FF ** -0.5, 0.15625, ((0, 4), (1, 4)))
    return {"tokens": tokens, "routes": routes, "router_weight": router_weight, "gate_weight": gate_weight, "up_weight": up_weight, "down_weight": down_weight}


def reference(tokens, routes, router_weight, gate_weight, up_weight, down_weight):
    rows_all = tokens.shape[0]
    logits = jnp.dot(tokens, router_weight, preferred_element_type=jnp.float32)
    chosen = jnp.take_along_axis(logits, routes, axis=1)
    raised = jnp.exp(chosen)
    gates = (raised / jnp.sum(raised, axis=1, keepdims=True)).astype(jnp.bfloat16)
    flat_ids = routes.reshape(-1).astype(jnp.int32)
    slots_all = flat_ids.shape[0]
    onehot = (flat_ids[:, None] == jnp.arange(EXPERTS, dtype=jnp.int32)[None, :]).astype(jnp.int32)
    blocked = onehot.reshape(N_SEC, ROWS_DEV * TOP, EXPERTS)
    before = jnp.cumsum(blocked, axis=1) - blocked
    position = jnp.sum(before * blocked, axis=2).reshape(-1).astype(jnp.int32)
    block_of = jnp.arange(slots_all, dtype=jnp.int32) // (ROWS_DEV * TOP)
    target = (block_of * CAP + position).astype(jnp.int32)
    table = jnp.full((EXPERTS, N_SEC * CAP), -1, jnp.int32)
    table = table.at[flat_ids, target].set(jnp.arange(slots_all, dtype=jnp.int32))
    gate_flat = gates.reshape(-1).astype(jnp.float32)

    def one_expert(total, inputs):
        column, w_gate, w_up, w_down = inputs
        valid = column >= 0
        source = jnp.maximum(column, 0).astype(jnp.int32)
        row_of = (source // TOP).astype(jnp.int32)
        picked = jnp.where(valid[:, None], tokens[row_of], jnp.zeros((), tokens.dtype))
        gate_part = jnp.dot(picked, w_gate, preferred_element_type=jnp.float32)
        up_part = jnp.dot(picked, w_up, preferred_element_type=jnp.float32)
        hidden = (jax.nn.silu(gate_part) * up_part).astype(jnp.bfloat16)
        blocks = hidden.reshape(-1, N_SUB, HSHARD).astype(jnp.float32)
        downs = w_down.reshape(N_SUB, HSHARD, D).astype(jnp.float32)
        parts = jnp.einsum("rqh,qhd->qrd", blocks, downs).astype(jnp.bfloat16)
        parts = lax.optimization_barrier(parts).astype(jnp.float32)
        summed = jnp.sum(parts, axis=0)
        weight = jnp.where(valid, gate_flat[source], jnp.zeros((), jnp.float32))
        total = total.at[row_of].add(weight[:, None] * summed)
        return total, None

    total, _ = lax.scan(one_expert, jnp.zeros((rows_all, D), jnp.float32),
                        (table, gate_weight, up_weight, down_weight))
    return total.astype(jnp.bfloat16)
```

```python
import jax
import jax.numpy as jnp
from jax import lax
from jax.experimental import pallas as pl
from jax.experimental.pallas import tpu as pltpu
from jax.sharding import PartitionSpec as P


def routed(tokens, routes, router_weight, gate_weight, up_weight, down_weight):
    rows, top = routes.shape
    experts = router_weight.shape[1]
    slots = 2 * rows * top // experts
    flat_ids = routes.reshape(-1)
    onehot = (flat_ids[:, None] == jnp.arange(experts, dtype=jnp.int32)[None, :]).astype(jnp.int32)
    before = jnp.cumsum(onehot, axis=0) - onehot
    position = jnp.sum(before * onehot, axis=1)
    target = flat_ids * slots + position
    placing = target[None, :] == jnp.arange(experts * slots, dtype=jnp.int32)[:, None]
    dispatch = jnp.sum(
        placing.reshape(experts * slots, rows, top).astype(jnp.int32), axis=2
    ).astype(jnp.bfloat16)
    full_rows = lax.all_gather(tokens, "sub", axis=1, tiled=True)
    logits = jnp.dot(full_rows, router_weight, preferred_element_type=jnp.float32)
    outgoing = jnp.dot(dispatch, full_rows, preferred_element_type=jnp.float32).astype(jnp.bfloat16)
    arrived = lax.all_to_all(
        outgoing.reshape(experts, slots, -1), "sec", split_axis=0, concat_axis=0, tiled=True
    )
    arrived = arrived.reshape(experts * slots, -1)
    chosen = jnp.sum(
        onehot.reshape(rows, top, experts).astype(jnp.float32) * logits[:, None, :], axis=2
    )
    raised = jnp.exp(chosen)
    gates = (raised / jnp.sum(raised, axis=1, keepdims=True)).astype(jnp.bfloat16)
    weighted = jnp.where(placing, gates.reshape(-1)[None, :], jnp.zeros((), jnp.bfloat16))
    combine = jnp.sum(
        weighted.reshape(experts * slots, rows, top).astype(jnp.float32), axis=2
    ).astype(jnp.bfloat16)
    gate_part = jnp.dot(arrived, gate_weight[0], preferred_element_type=jnp.float32)
    up_part = jnp.dot(arrived, up_weight[0], preferred_element_type=jnp.float32)
    hidden = (jax.nn.silu(gate_part) * up_part).astype(jnp.bfloat16)
    partial_value = jnp.dot(hidden, down_weight[0], preferred_element_type=jnp.float32).astype(
        jnp.bfloat16
    )
    contract = (((0,), (0,)), ((), ()))
    returned = lax.all_to_all(
        partial_value.reshape(experts, slots, -1), "sec", split_axis=0, concat_axis=0, tiled=True
    )
    returned = returned.reshape(experts * slots, -1)
    combined = lax.dot_general(combine, returned, contract, preferred_element_type=jnp.float32)
    mixed = lax.psum_scatter(combined.astype(jnp.bfloat16), "sub", scatter_dimension=1, tiled=True)
    return mixed


def flip(index, step):
    if step == 0:
        return index
    if step == 1:
        return index + 1 - 2 * (index % 2)
    if step == 2:
        return (index + 2) % 4
    return 3 - index


def kernel(
    tokens, routes, router, gate_w, up_w, down_w, out,
    x, wide, down, keep, core_out, core_in, side_out, side_in, far_out, far_in,
    load_sem, send_sem, recv_sem,
):
    group, sec, sub = (lax.axis_index(name) for name in ("group", "sec", "sub"))
    width = tokens.shape[1]
    hidden_units = gate_w.shape[2]
    rows, top = tokens.shape[0], routes.shape[0]

    loads = [pltpu.make_async_copy(tokens, x.at[0, 0], load_sem.at[0])]
    for j in range(4):
        part = pl.ds(pl.multiple_of(flip(sub, j) * width, width), width)
        loads.append(
            pltpu.make_async_copy(
                gate_w.at[0, part, :], wide.at[j, :, pl.ds(0, hidden_units)], load_sem.at[1 + j]
            )
        )
        loads.append(
            pltpu.make_async_copy(
                up_w.at[0, part, :], wide.at[j, :, pl.ds(hidden_units, hidden_units)],
                load_sem.at[5 + j],
            )
        )
    for j in range(4):
        part = pl.ds(pl.multiple_of(flip(sub, j) * width, width), width)
        loads.append(pltpu.make_async_copy(down_w.at[0, :, part], down.at[j], load_sem.at[9 + j]))
    for load in loads:
        load.start()

    barrier = pltpu.get_barrier_semaphore()
    partners = [(group, flip(sec, k), sub) for k in (1, 2, 3)]
    partners += [(group, sec, flip(sub, j)) for j in (1, 2)]
    for partner in partners:
        pl.semaphore_signal(
            barrier, inc=1, device_id=partner, device_id_type=pl.DeviceIdType.MESH
        )
    pl.semaphore_wait(barrier, len(partners))

    def copy(source, target, number, over_sec, over_sub):
        return pltpu.make_async_remote_copy(
            src_ref=source,
            dst_ref=target,
            send_sem=send_sem.at[number],
            recv_sem=recv_sem.at[number],
            device_id=(group, flip(sec, over_sec), flip(sub, over_sub)),
            device_id_type=pl.DeviceIdType.MESH,
        )

    gather_far = [None] + [copy(x.at[0, 0], x.at[k, 0], k, k, 0) for k in (1, 2, 3)]
    gather_core = [copy(x.at[k, 0], x.at[k, 1], 4 + k, 0, 1) for k in range(4)]
    gather_side = [copy(x.at[k, 0], x.at[k, 2], 8 + k, 0, 2) for k in range(4)]
    gather_last = [copy(x.at[k, 2], x.at[k, 3], 12 + k, 0, 1) for k in range(4)]
    sum_core = [copy(core_out.at[k], core_in.at[k], 16 + k, 0, 1) for k in range(4)]
    sum_side = [copy(side_out.at[k], side_in.at[k], 20 + k, 0, 2) for k in range(4)]
    sum_far = [None] + [copy(far_out.at[k], far_in.at[k], 24 + k, k, 0) for k in (1, 2, 3)]

    loads[0].wait()
    gather_side[0].start()
    for k in (1, 2, 3):
        gather_far[k].start()
    gather_core[0].start()

    def pass_on(k):
        gather_far[k].wait_recv()
        gather_side[k].start()
        gather_core[k].start()

    def pass_last(k):
        gather_side[k].wait_recv()
        gather_last[k].start()

    def expert(k):
        gather_core[k].wait_recv()
        gather_last[k].wait_recv()
        both = jnp.dot(x[k, 0], wide[0], preferred_element_type=jnp.float32)
        for j in (1, 2, 3):
            both += jnp.dot(x[k, j], wide[j], preferred_element_type=jnp.float32)
        hidden = (jax.nn.silu(both[:, :hidden_units]) * both[:, hidden_units:]).astype(jnp.bfloat16)
        if k == 0:
            for load in loads[9:]:
                load.wait()
        for place, j in enumerate((1, 3)):
            core_out[k, place] = jnp.dot(
                hidden, down[j], preferred_element_type=jnp.float32
            ).astype(jnp.bfloat16)
        sum_core[k].start()
        for place, j in enumerate((0, 2)):
            keep[k, place] = jnp.dot(hidden, down[j], preferred_element_type=jnp.float32)

    def to_side(k):
        sum_core[k].wait_recv()
        side_out[k] = (keep[k, 1] + core_in[k, 1].astype(jnp.float32)).astype(jnp.bfloat16)
        sum_side[k].start()
        keep[k, 0] = keep[k, 0] + core_in[k, 0].astype(jnp.float32)

    def to_far(k):
        sum_side[k].wait_recv()
        total = keep[k, 0] + side_in[k].astype(jnp.float32)
        if k == 0:
            keep[k, 0] = total
        else:
            far_out[k] = total.astype(jnp.bfloat16)
            sum_far[k].start()

    def gates():
        logits = jnp.zeros((router.shape[0], rows), jnp.float32)
        for j in range(4):
            part = pl.ds(pl.multiple_of(flip(sub, j) * width, width), width)
            logits += lax.dot_general(
                router[:, part], x[0, j], (((1,), (1,)), ((), ())),
                preferred_element_type=jnp.float32,
            )
        names = [routes[t : t + 1, :] for t in range(top)]
        raised = []
        for t in range(top):
            chosen = jnp.zeros((1, rows), jnp.float32)
            for e in range(router.shape[0]):
                chosen = jnp.where(names[t] == e, logits[e : e + 1, :], chosen)
            raised.append(jnp.exp(chosen))
        whole = sum(raised)
        shares = [(r / whole).astype(jnp.bfloat16).astype(jnp.float32) for r in raised]
        lines = []
        for k in range(4):
            line = jnp.zeros((1, rows), jnp.float32)
            for t in range(top):
                line += jnp.where(names[t] == flip(sec, k), shares[t], 0.0)
            lines.append(line)
        lines.append(jnp.zeros((4, rows), jnp.float32))
        return jnp.transpose(jnp.concatenate(lines, axis=0))

    pass_last(0)
    pass_on(1)
    for load in loads[1:9]:
        load.wait()
    expert(0)
    pass_last(1)
    pass_on(2)
    to_side(0)
    expert(1)
    pass_last(2)
    pass_on(3)
    to_side(1)
    to_far(0)
    expert(2)
    pass_last(3)
    to_side(2)
    to_far(1)
    expert(3)
    to_far(2)
    weights = gates()
    to_side(3)
    mixed = weights[:, 0:1] * keep[0, 0]
    to_far(3)
    for k in (1, 2, 3):
        sum_far[k].wait_recv()
        mixed += weights[:, k : k + 1] * far_in[k].astype(jnp.float32)
    out[...] = mixed.astype(jnp.bfloat16)
    for k in range(4):
        gather_core[k].wait_send()
        gather_side[k].wait_send()
        gather_last[k].wait_send()
        sum_core[k].wait_send()
        sum_side[k].wait_send()
        if k > 0:
            gather_far[k].wait_send()
            sum_far[k].wait_send()


def dense(tokens, routes, router_weight, gate_weight, up_weight, down_weight):
    rows, width = tokens.shape
    hidden_units = gate_weight.shape[2]
    hbm, vmem = pl.BlockSpec(memory_space=pl.ANY), pl.BlockSpec(memory_space=pltpu.VMEM)
    block = (rows, width)
    return pl.pallas_call(
        kernel,
        out_shape=jax.ShapeDtypeStruct(block, jnp.bfloat16),
        in_specs=[hbm, vmem, vmem, hbm, hbm, hbm],
        out_specs=vmem,
        scratch_shapes=[
            pltpu.VMEM((4, 4) + block, jnp.bfloat16),
            pltpu.VMEM((4, width, 2 * hidden_units), jnp.bfloat16),
            pltpu.VMEM((4, hidden_units, width), jnp.bfloat16),
            pltpu.VMEM((4, 2) + block, jnp.float32),
            pltpu.VMEM((4, 2) + block, jnp.bfloat16),
            pltpu.VMEM((4, 2) + block, jnp.bfloat16),
            pltpu.VMEM((4,) + block, jnp.bfloat16),
            pltpu.VMEM((4,) + block, jnp.bfloat16),
            pltpu.VMEM((4,) + block, jnp.bfloat16),
            pltpu.VMEM((4,) + block, jnp.bfloat16),
            pltpu.SemaphoreType.DMA((13,)),
            pltpu.SemaphoreType.DMA((28,)),
            pltpu.SemaphoreType.DMA((28,)),
        ],
        compiler_params=pltpu.CompilerParams(
            collective_id=0, has_side_effects=True, vmem_limit_bytes=40 * 2**20
        ),
    )(tokens, routes.T, router_weight.T, gate_weight, up_weight, down_weight)


def solution(mesh):
    def local(*args):
        tokens, routes, router_weight = args[:3]
        rows, top = routes.shape
        experts = router_weight.shape[1]
        sec, sub = mesh.shape["sec"], mesh.shape["sub"]
        if experts == sec == sub == 4 and 2 * rows * top // experts >= rows and rows % 16 == 0:
            return dense(*args)
        return routed(*args)

    placed = (
        P(("group", "sec"), "sub"),
        P(("group", "sec"), None),
        P(),
        P("sec", None, "sub"),
        P("sec", None, "sub"),
        P("sec", "sub", None),
    )
    return jax.shard_map(
        local, mesh=mesh, in_specs=placed, out_specs=P(("group", "sec"), "sub"), check_vma=False
    )
```

```python
import functools
import jax
import jax.numpy as jnp
from jax import lax
from jax.experimental import pallas as pl
from jax.experimental.pallas import tpu as pltpu
from jax.sharding import PartitionSpec as P


def routed(tokens, routes, router_weight, gate_weight, up_weight, down_weight):
    rows, top = routes.shape
    experts = router_weight.shape[1]
    slots = 2 * rows * top // experts
    flat_ids = routes.reshape(-1)
    onehot = (flat_ids[:, None] == jnp.arange(experts, dtype=jnp.int32)[None, :]).astype(jnp.int32)
    before = jnp.cumsum(onehot, axis=0) - onehot
    position = jnp.sum(before * onehot, axis=1)
    target = flat_ids * slots + position
    placing = target[None, :] == jnp.arange(experts * slots, dtype=jnp.int32)[:, None]
    dispatch = jnp.sum(
        placing.reshape(experts * slots, rows, top).astype(jnp.int32), axis=2
    ).astype(jnp.bfloat16)
    full_rows = lax.all_gather(tokens, "sub", axis=1, tiled=True)
    logits = jnp.dot(full_rows, router_weight, preferred_element_type=jnp.float32)
    outgoing = jnp.dot(dispatch, full_rows, preferred_element_type=jnp.float32).astype(jnp.bfloat16)
    arrived = lax.all_to_all(
        outgoing.reshape(experts, slots, -1), "sec", split_axis=0, concat_axis=0, tiled=True
    )
    arrived = arrived.reshape(experts * slots, -1)
    chosen = jnp.sum(
        onehot.reshape(rows, top, experts).astype(jnp.float32) * logits[:, None, :], axis=2
    )
    raised = jnp.exp(chosen)
    gates = (raised / jnp.sum(raised, axis=1, keepdims=True)).astype(jnp.bfloat16)
    weighted = jnp.where(placing, gates.reshape(-1)[None, :], jnp.zeros((), jnp.bfloat16))
    combine = jnp.sum(
        weighted.reshape(experts * slots, rows, top).astype(jnp.float32), axis=2
    ).astype(jnp.bfloat16)
    gate_part = jnp.dot(arrived, gate_weight[0], preferred_element_type=jnp.float32)
    up_part = jnp.dot(arrived, up_weight[0], preferred_element_type=jnp.float32)
    hidden = (jax.nn.silu(gate_part) * up_part).astype(jnp.bfloat16)
    partial_value = jnp.dot(hidden, down_weight[0], preferred_element_type=jnp.float32).astype(
        jnp.bfloat16
    )
    contract = (((0,), (0,)), ((), ()))
    returned = lax.all_to_all(
        partial_value.reshape(experts, slots, -1), "sec", split_axis=0, concat_axis=0, tiled=True
    )
    returned = returned.reshape(experts * slots, -1)
    combined = lax.dot_general(combine, returned, contract, preferred_element_type=jnp.float32)
    mixed = lax.psum_scatter(combined.astype(jnp.bfloat16), "sub", scatter_dimension=1, tiled=True)
    return mixed


PIECES = 2


def flip(index, step):
    if step == 0:
        return index
    if step == 1:
        return index + 1 - 2 * (index % 2)
    if step == 2:
        return (index + 2) % 4
    return 3 - index


def kernel(
    tokens, routes_hbm, router_hbm, gate_w, up_w, down_w, out,
    routes, router, x, wide, down, keep, core_out, core_in, side_out, side_in, far_out, far_in,
    load_sem, send_sem, recv_sem,
):
    group, sec, sub = (lax.axis_index(name) for name in ("group", "sec", "sub"))
    width = tokens.shape[1]
    hidden_units = gate_w.shape[2]
    rows, top = tokens.shape[0], routes.shape[0]
    experts = router.shape[0]

    loads = [pltpu.make_async_copy(tokens, x.at[0, 0], load_sem.at[0])]
    for j in range(4):
        part = pl.ds(pl.multiple_of(flip(sub, j) * width, width), width)
        loads.append(
            pltpu.make_async_copy(
                gate_w.at[0, part, :], wide.at[j, :, pl.ds(0, hidden_units)], load_sem.at[1 + j]
            )
        )
        loads.append(
            pltpu.make_async_copy(
                up_w.at[0, part, :], wide.at[j, :, pl.ds(hidden_units, hidden_units)],
                load_sem.at[5 + j],
            )
        )
    for j in range(4):
        part = pl.ds(pl.multiple_of(flip(sub, j) * width, width), width)
        loads.append(pltpu.make_async_copy(down_w.at[0, :, part], down.at[j], load_sem.at[9 + j]))
    loads.append(pltpu.make_async_copy(routes_hbm, routes, load_sem.at[13]))
    loads.append(pltpu.make_async_copy(router_hbm, router, load_sem.at[14]))
    for load in loads:
        load.start()

    barrier = pltpu.get_barrier_semaphore()
    partners = [(group, flip(sec, k), sub) for k in (1, 2, 3)]
    partners += [(group, sec, flip(sub, j)) for j in (1, 2)]
    for partner in partners:
        pl.semaphore_signal(
            barrier, inc=1, device_id=partner, device_id_type=pl.DeviceIdType.MESH
        )
    pl.semaphore_wait(barrier, len(partners))

    used = [0]

    def copy(source, target, over_sec, over_sub):
        number = used[0]
        used[0] += 1
        return pltpu.make_async_remote_copy(
            src_ref=source,
            dst_ref=target,
            send_sem=send_sem.at[number],
            recv_sem=recv_sem.at[number],
            device_id=(group, flip(sec, over_sec), flip(sub, over_sub)),
            device_id_type=pl.DeviceIdType.MESH,
        )

    cuts = [pl.ds(h * (rows // PIECES), rows // PIECES) for h in range(PIECES)]

    def copies(source, target, over_sec, over_sub):
        return [copy(source.at[cut], target.at[cut], over_sec, over_sub) for cut in cuts]

    gather_far = {k: copies(x.at[0, 0], x.at[k, 0], k, 0) for k in (1, 2, 3)}
    gather_far["twin"] = copies(x.at[0, 2], x.at[1, 2], 1, 0)
    gather_core = {k: copies(x.at[k, 0], x.at[k, 1], 0, 1) for k in range(4)}
    gather_side = {k: copies(x.at[k, 0], x.at[k, 2], 0, 2) for k in (0, 2, 3)}
    gather_last = {k: copies(x.at[k, 2], x.at[k, 3], 0, 1) for k in range(4)}
    sum_core = {k: copy(core_out.at[k], core_in.at[k], 0, 1) for k in range(4)}
    sum_side = {k: copies(side_out.at[k], side_in.at[k], 0, 2) for k in (0, 2, 3)}
    sum_far = {k: copies(far_out.at[k], far_in.at[k], k, 0) for k in (1, 2, 3)}
    sum_far["twin"] = copies(far_out.at[0], far_in.at[0], 1, 0)
    every = range(PIECES)

    def pass_on(k, h):
        gather_far[k][h].wait_recv()
        if k != 1:
            gather_side[k][h].start()
        gather_core[k][h].start()

    def pass_last(k, h):
        (gather_far["twin"] if k == 1 else gather_side[k])[h].wait_recv()
        gather_last[k][h].start()

    def expert(k):
        for h in every:
            gather_core[k][h].wait_recv()
            gather_last[k][h].wait_recv()
        both = jnp.dot(x[k, 0], wide[0], preferred_element_type=jnp.float32)
        for j in (1, 2, 3):
            both += jnp.dot(x[k, j], wide[j], preferred_element_type=jnp.float32)
        hidden = (jax.nn.silu(both[:, :hidden_units]) * both[:, hidden_units:]).astype(jnp.bfloat16)
        if k == 0:
            for load in loads[9:13]:
                load.wait()
        for place, j in enumerate((1, 3)):
            core_out[k, place] = jnp.dot(
                hidden, down[j], preferred_element_type=jnp.float32
            ).astype(jnp.bfloat16)
        sum_core[k].start()
        for place, j in enumerate((0, 2)):
            keep[k, place] = jnp.dot(hidden, down[j], preferred_element_type=jnp.float32)

    def to_side(k):
        sum_core[k].wait_recv()
        for h in every:
            side_out[k, cuts[h]] = (
                keep[k, 1, cuts[h]] + core_in[k, 1, cuts[h]].astype(jnp.float32)
            ).astype(jnp.bfloat16)
            sum_side[k][h].start()

    def to_far(k, h):
        sum_side[k][h].wait_recv()
        far_out[k, cuts[h]] = (
            keep[k, 0, cuts[h]]
            + core_in[k, 0, cuts[h]].astype(jnp.float32)
            + side_in[k, cuts[h]].astype(jnp.float32)
        ).astype(jnp.bfloat16)
        sum_far[k][h].start()

    def both_to_next():
        sum_core[1].wait_recv()
        for place, slot, name in ((1, 0, "twin"), (0, 1, 1)):
            for h in every:
                far_out[slot, cuts[h]] = (
                    keep[1, place, cuts[h]] + core_in[1, place, cuts[h]].astype(jnp.float32)
                ).astype(jnp.bfloat16)
                sum_far[name][h].start()

    def gates():
        loads[13].wait()
        loads[14].wait()
        logits = jnp.zeros((experts, rows), jnp.float32)
        for j in range(4):
            part = pl.ds(pl.multiple_of(flip(sub, j) * width, width), width)
            logits += lax.dot_general(
                router[:, part], x[0, j], (((1,), (1,)), ((), ())),
                preferred_element_type=jnp.float32,
            )
        names = [routes[t : t + 1, :] for t in range(top)]
        raised = []
        for t in range(top):
            chosen = jnp.zeros((1, rows), jnp.float32)
            for e in range(experts):
                chosen = jnp.where(names[t] == e, logits[e : e + 1, :], chosen)
            raised.append(jnp.exp(chosen))
        whole = sum(raised)
        shares = [(r / whole).astype(jnp.bfloat16).astype(jnp.float32) for r in raised]
        lines = []
        for k in range(4):
            line = jnp.zeros((1, rows), jnp.float32)
            for t in range(top):
                line += jnp.where(names[t] == flip(sec, k), shares[t], 0.0)
            lines.append(line)
        lines.append(jnp.zeros((4, rows), jnp.float32))
        return jnp.transpose(jnp.concatenate(lines, axis=0))

    loads[0].wait()
    for h in every:
        gather_side[0][h].start()
        gather_far[2][h].start()
    for h in every:
        gather_core[0][h].start()
    for h in every:
        gather_far[1][h].start()
    for h in range(PIECES - 1):
        gather_far[2][h].wait_send()
        gather_far[3][h].start()
    for h in every:
        pass_last(0, h)
        gather_far["twin"][h].start()
    for h in every:
        pass_on(2, h)
    gather_far[2][PIECES - 1].wait_send()
    gather_far[3][PIECES - 1].start()
    for h in every:
        pass_on(1, h)
    for load in loads[1:9]:
        load.wait()
    expert(0)
    for h in every:
        pass_on(3, h)
        pass_last(2, h)
        pass_last(1, h)
    expert(2)
    expert(1)
    to_side(2)
    for h in every:
        pass_last(3, h)
    both_to_next()
    expert(3)
    to_side(3)
    for h in every:
        to_far(2, h)
    weights = gates()
    sum_core[0].wait_recv()
    first, second = weights[:, 0:1], weights[:, 1:2]
    for h in every:
        sum_far["twin"][h].wait_recv()
    side_out[0] = (
        first * (keep[0, 1] + core_in[0, 1].astype(jnp.float32))
        + second * far_in[0].astype(jnp.float32)
    ).astype(jnp.bfloat16)
    for h in every:
        sum_side[0][h].start()
    for h in every:
        to_far(3, h)
    for h in every:
        sum_far[1][h].wait_recv()
    mixed = (
        first * (keep[0, 0] + core_in[0, 0].astype(jnp.float32))
        + second * far_in[1].astype(jnp.float32)
    )
    for h in every:
        sum_far[2][h].wait_recv()
    mixed += weights[:, 2:3] * far_in[2].astype(jnp.float32)
    for h in every:
        sum_side[0][h].wait_recv()
    mixed += side_in[0].astype(jnp.float32)
    for h in every:
        sum_far[3][h].wait_recv()
    out[...] = (mixed + weights[:, 3:4] * far_in[3].astype(jnp.float32)).astype(jnp.bfloat16)
    for family in (gather_far, gather_core, gather_side, gather_last, sum_side, sum_far):
        for name in family:
            for h in every:
                if family is not gather_far or name != 2:
                    family[name][h].wait_send()
    for k in range(4):
        sum_core[k].wait_send()


def dense(tokens, routes, router_weight, gate_weight, up_weight, down_weight):
    rows, width = tokens.shape
    hidden_units = gate_weight.shape[2]
    hbm, vmem = pl.BlockSpec(memory_space=pltpu.HBM), pl.BlockSpec(memory_space=pltpu.VMEM)
    block = (rows, width)
    return pl.pallas_call(
        kernel,
        out_shape=jax.ShapeDtypeStruct(block, jnp.bfloat16),
        in_specs=[hbm] * 6,
        out_specs=vmem,
        scratch_shapes=[
            pltpu.VMEM(routes.shape[::-1], routes.dtype),
            pltpu.VMEM(router_weight.shape[::-1], router_weight.dtype),
            pltpu.VMEM((4, 4) + block, jnp.bfloat16),
            pltpu.VMEM((4, width, 2 * hidden_units), jnp.bfloat16),
            pltpu.VMEM((4, hidden_units, width), jnp.bfloat16),
            pltpu.VMEM((4, 2) + block, jnp.float32),
            pltpu.VMEM((4, 2) + block, jnp.bfloat16),
            pltpu.VMEM((4, 2) + block, jnp.bfloat16),
            pltpu.VMEM((4,) + block, jnp.bfloat16),
            pltpu.VMEM((4,) + block, jnp.bfloat16),
            pltpu.VMEM((4,) + block, jnp.bfloat16),
            pltpu.VMEM((4,) + block, jnp.bfloat16),
            pltpu.SemaphoreType.DMA((15,)),
            pltpu.SemaphoreType.DMA((22 * PIECES + 4,)),
            pltpu.SemaphoreType.DMA((22 * PIECES + 4,)),
        ],
        compiler_params=pltpu.CompilerParams(
            collective_id=0, has_side_effects=True, vmem_limit_bytes=60 * 2**20
        ),
    )(tokens, routes.T, router_weight.T, gate_weight, up_weight, down_weight)


def solution(mesh):
    def local(*args):
        tokens, routes, router_weight = args[:3]
        rows, top = routes.shape
        experts = router_weight.shape[1]
        sec, sub = mesh.shape["sec"], mesh.shape["sub"]
        if experts == sec == sub == 4 and 2 * rows * top // experts >= rows and rows % 16 == 0:
            return dense(*args)
        return routed(*args)

    placed = (
        P(("group", "sec"), "sub"),
        P(("group", "sec"), None),
        P(),
        P("sec", None, "sub"),
        P("sec", None, "sub"),
        P("sec", "sub", None),
    )
    return jax.shard_map(
        local, mesh=mesh, in_specs=placed, out_specs=P(("group", "sec"), "sub"), check_vma=False
    )
```

```python
import functools
import jax
import jax.numpy as jnp
from jax import lax
from jax.experimental import pallas as pl
from jax.experimental.pallas import tpu as pltpu
from jax.sharding import PartitionSpec as P


def routed(tokens, routes, router_weight, gate_weight, up_weight, down_weight):
    rows, top = routes.shape
    experts = router_weight.shape[1]
    slots = 2 * rows * top // experts
    flat_ids = routes.reshape(-1)
    onehot = (flat_ids[:, None] == jnp.arange(experts, dtype=jnp.int32)[None, :]).astype(jnp.int32)
    before = jnp.cumsum(onehot, axis=0) - onehot
    position = jnp.sum(before * onehot, axis=1)
    target = flat_ids * slots + position
    placing = target[None, :] == jnp.arange(experts * slots, dtype=jnp.int32)[:, None]
    dispatch = jnp.sum(
        placing.reshape(experts * slots, rows, top).astype(jnp.int32), axis=2
    ).astype(jnp.bfloat16)
    full_rows = lax.all_gather(tokens, "sub", axis=1, tiled=True)
    logits = jnp.dot(full_rows, router_weight, preferred_element_type=jnp.float32)
    outgoing = jnp.dot(dispatch, full_rows, preferred_element_type=jnp.float32).astype(jnp.bfloat16)
    arrived = lax.all_to_all(
        outgoing.reshape(experts, slots, -1), "sec", split_axis=0, concat_axis=0, tiled=True
    )
    arrived = arrived.reshape(experts * slots, -1)
    chosen = jnp.sum(
        onehot.reshape(rows, top, experts).astype(jnp.float32) * logits[:, None, :], axis=2
    )
    raised = jnp.exp(chosen)
    gates = (raised / jnp.sum(raised, axis=1, keepdims=True)).astype(jnp.bfloat16)
    weighted = jnp.where(placing, gates.reshape(-1)[None, :], jnp.zeros((), jnp.bfloat16))
    combine = jnp.sum(
        weighted.reshape(experts * slots, rows, top).astype(jnp.float32), axis=2
    ).astype(jnp.bfloat16)
    gate_part = jnp.dot(arrived, gate_weight[0], preferred_element_type=jnp.float32)
    up_part = jnp.dot(arrived, up_weight[0], preferred_element_type=jnp.float32)
    hidden = (jax.nn.silu(gate_part) * up_part).astype(jnp.bfloat16)
    partial_value = jnp.dot(hidden, down_weight[0], preferred_element_type=jnp.float32).astype(
        jnp.bfloat16
    )
    contract = (((0,), (0,)), ((), ()))
    returned = lax.all_to_all(
        partial_value.reshape(experts, slots, -1), "sec", split_axis=0, concat_axis=0, tiled=True
    )
    returned = returned.reshape(experts * slots, -1)
    combined = lax.dot_general(combine, returned, contract, preferred_element_type=jnp.float32)
    mixed = lax.psum_scatter(combined.astype(jnp.bfloat16), "sub", scatter_dimension=1, tiled=True)
    return mixed


PIECES = 2


def flip(index, step):
    if step == 0:
        return index
    if step == 1:
        return index + 1 - 2 * (index % 2)
    if step == 2:
        return (index + 2) % 4
    return 3 - index


def kernel(
    tokens, routes_hbm, router_hbm, gate_w, up_w, down_w, out,
    routes, router, x, wide, down, keep, core_out, core_in, side_out, side_in, far_out, far_in,
    load_sem, send_sem, recv_sem,
):
    group, sec, sub = (lax.axis_index(name) for name in ("group", "sec", "sub"))
    width = tokens.shape[1]
    hidden_units = gate_w.shape[2]
    rows, top = tokens.shape[0], routes.shape[0]
    experts = router.shape[0]

    loads = [pltpu.make_async_copy(tokens, x.at[0, 0], load_sem.at[0])]
    for j in range(4):
        part = pl.ds(pl.multiple_of(flip(sub, j) * width, width), width)
        loads.append(
            pltpu.make_async_copy(
                gate_w.at[0, part, :], wide.at[j, :, pl.ds(0, hidden_units)], load_sem.at[1 + j]
            )
        )
        loads.append(
            pltpu.make_async_copy(
                up_w.at[0, part, :], wide.at[j, :, pl.ds(hidden_units, hidden_units)],
                load_sem.at[5 + j],
            )
        )
    for j in range(4):
        part = pl.ds(pl.multiple_of(flip(sub, j) * width, width), width)
        loads.append(pltpu.make_async_copy(down_w.at[0, :, part], down.at[j], load_sem.at[9 + j]))
    loads.append(pltpu.make_async_copy(routes_hbm, routes, load_sem.at[13]))
    loads.append(pltpu.make_async_copy(router_hbm, router, load_sem.at[14]))
    for load in loads:
        load.start()

    barrier = pltpu.get_barrier_semaphore()
    partners = [(group, flip(sec, k), sub) for k in (1, 2, 3)]
    partners += [(group, sec, flip(sub, j)) for j in (1, 2)]
    for partner in partners:
        pl.semaphore_signal(
            barrier, inc=1, device_id=partner, device_id_type=pl.DeviceIdType.MESH
        )
    pl.semaphore_wait(barrier, len(partners))

    used = [0]

    def copy(source, target, over_sec, over_sub, landing=None):
        number = used[0]
        used[0] += 1
        return pltpu.make_async_remote_copy(
            src_ref=source,
            dst_ref=target,
            send_sem=send_sem.at[number],
            recv_sem=recv_sem.at[number if landing is None else landing],
            device_id=(group, flip(sec, over_sec), flip(sub, over_sub)),
            device_id_type=pl.DeviceIdType.MESH,
        )

    cuts = [pl.ds(h * (rows // PIECES), rows // PIECES) for h in range(PIECES)]

    def copies(source, target, over_sec, over_sub):
        return [copy(source.at[cut], target.at[cut], over_sec, over_sub) for cut in cuts]

    gather_far = {k: copies(x.at[0, 0], x.at[k, 0], k, 0) for k in (1, 2, 3)}
    gather_far["twin"] = copies(x.at[0, 2], x.at[1, 2], 1, 0)
    relay = [
        copy(x.at[2, 0].at[cut], x.at[3, 0].at[cut], 1, 0, 2 * PIECES + h)
        for h, cut in enumerate(cuts)
    ]
    gather_core = {k: copies(x.at[k, 0], x.at[k, 1], 0, 1) for k in range(4)}
    gather_side = {k: copies(x.at[k, 0], x.at[k, 2], 0, 2) for k in (0, 2, 3)}
    gather_last = {k: copies(x.at[k, 2], x.at[k, 3], 0, 1) for k in range(4)}
    sum_core = {k: copy(core_out.at[k], core_in.at[k], 0, 1) for k in range(4)}
    sum_side = {k: copies(side_out.at[k], side_in.at[k], 0, 2) for k in (0, 2, 3)}
    sum_far = {k: copies(far_out.at[k], far_in.at[k], k, 0) for k in (1, 2, 3)}
    sum_far["twin"] = copies(far_out.at[0], far_in.at[0], 1, 0)
    every = range(PIECES)

    def pass_on(k, h):
        gather_far[k][h].wait_recv()
        if k == 2:

            @pl.when(inner)
            def _():
                relay[h].start()

        if k != 1:
            gather_side[k][h].start()
        gather_core[k][h].start()

    def pass_last(k, h):
        (gather_far["twin"] if k == 1 else gather_side[k])[h].wait_recv()
        gather_last[k][h].start()

    def expert(k):
        for h in every:
            gather_core[k][h].wait_recv()
            gather_last[k][h].wait_recv()
        both = jnp.dot(x[k, 0], wide[0], preferred_element_type=jnp.float32)
        for j in (1, 2, 3):
            both += jnp.dot(x[k, j], wide[j], preferred_element_type=jnp.float32)
        hidden = (jax.nn.silu(both[:, :hidden_units]) * both[:, hidden_units:]).astype(jnp.bfloat16)
        if k == 0:
            for load in loads[9:13]:
                load.wait()
        for place, j in enumerate((1, 3)):
            core_out[k, place] = jnp.dot(
                hidden, down[j], preferred_element_type=jnp.float32
            ).astype(jnp.bfloat16)
        sum_core[k].start()
        for place, j in enumerate((0, 2)):
            keep[k, place] = jnp.dot(hidden, down[j], preferred_element_type=jnp.float32)

    def to_side(k):
        sum_core[k].wait_recv()
        for h in every:
            side_out[k, cuts[h]] = (
                keep[k, 1, cuts[h]] + core_in[k, 1, cuts[h]].astype(jnp.float32)
            ).astype(jnp.bfloat16)
            sum_side[k][h].start()

    def to_far(k, h):
        sum_side[k][h].wait_recv()
        far_out[k, cuts[h]] = (
            keep[k, 0, cuts[h]]
            + core_in[k, 0, cuts[h]].astype(jnp.float32)
            + side_in[k, cuts[h]].astype(jnp.float32)
        ).astype(jnp.bfloat16)
        sum_far[k][h].start()

    def both_to_next():
        sum_core[1].wait_recv()
        for place, slot, name in ((1, 0, "twin"), (0, 1, 1)):
            for h in every:
                far_out[slot, cuts[h]] = (
                    keep[1, place, cuts[h]] + core_in[1, place, cuts[h]].astype(jnp.float32)
                ).astype(jnp.bfloat16)
                sum_far[name][h].start()

    def gates():
        loads[13].wait()
        loads[14].wait()
        logits = jnp.zeros((experts, rows), jnp.float32)
        for j in range(4):
            part = pl.ds(pl.multiple_of(flip(sub, j) * width, width), width)
            logits += lax.dot_general(
                router[:, part], x[0, j], (((1,), (1,)), ((), ())),
                preferred_element_type=jnp.float32,
            )
        names = [routes[t : t + 1, :] for t in range(top)]
        raised = []
        for t in range(top):
            chosen = jnp.zeros((1, rows), jnp.float32)
            for e in range(experts):
                chosen = jnp.where(names[t] == e, logits[e : e + 1, :], chosen)
            raised.append(jnp.exp(chosen))
        whole = sum(raised)
        shares = [(r / whole).astype(jnp.bfloat16).astype(jnp.float32) for r in raised]
        lines = []
        for k in range(4):
            line = jnp.zeros((1, rows), jnp.float32)
            for t in range(top):
                line += jnp.where(names[t] == flip(sec, k), shares[t], 0.0)
            lines.append(line)
        lines.append(jnp.zeros((4, rows), jnp.float32))
        return jnp.transpose(jnp.concatenate(lines, axis=0))

    loads[0].wait()
    for h in every:
        gather_side[0][h].start()
        gather_far[2][h].start()
    for h in every:
        gather_core[0][h].start()
    for h in every:
        gather_far[1][h].start()
    inner = jnp.logical_or(sec == 1, sec == 2)

    @pl.when(inner)
    def _():
        for h in every:
            gather_far[3][h].start()

    for h in every:
        pass_last(0, h)
        gather_far["twin"][h].start()
    for h in every:
        pass_on(2, h)
    for h in every:
        pass_on(1, h)
    for load in loads[1:9]:
        load.wait()
    expert(0)
    for h in every:
        pass_on(3, h)
        pass_last(2, h)
        pass_last(1, h)
    expert(2)
    expert(1)
    to_side(2)
    for h in every:
        pass_last(3, h)
    both_to_next()
    expert(3)
    to_side(3)
    for h in every:
        to_far(2, h)
    weights = gates()
    sum_core[0].wait_recv()
    first, second = weights[:, 0:1], weights[:, 1:2]
    for h in every:
        sum_far["twin"][h].wait_recv()
    side_out[0] = (
        first * (keep[0, 1] + core_in[0, 1].astype(jnp.float32))
        + second * far_in[0].astype(jnp.float32)
    ).astype(jnp.bfloat16)
    for h in every:
        sum_side[0][h].start()
    for h in every:
        to_far(3, h)
    for h in every:
        sum_far[1][h].wait_recv()
    mixed = (
        first * (keep[0, 0] + core_in[0, 0].astype(jnp.float32))
        + second * far_in[1].astype(jnp.float32)
    )
    for h in every:
        sum_far[2][h].wait_recv()
    mixed += weights[:, 2:3] * far_in[2].astype(jnp.float32)
    for h in every:
        sum_side[0][h].wait_recv()
    mixed += side_in[0].astype(jnp.float32)
    for h in every:
        sum_far[3][h].wait_recv()
    out[...] = (mixed + weights[:, 3:4] * far_in[3].astype(jnp.float32)).astype(jnp.bfloat16)
    for family in (gather_far, gather_core, gather_side, gather_last, sum_side, sum_far):
        for name in family:
            if family is gather_far and name == 3:
                continue
            for h in every:
                family[name][h].wait_send()

    @pl.when(inner)
    def _():
        for h in every:
            gather_far[3][h].wait_send()
            relay[h].wait_send()

    for k in range(4):
        sum_core[k].wait_send()


def dense(tokens, routes, router_weight, gate_weight, up_weight, down_weight):
    rows, width = tokens.shape
    hidden_units = gate_weight.shape[2]
    hbm, vmem = pl.BlockSpec(memory_space=pltpu.HBM), pl.BlockSpec(memory_space=pltpu.VMEM)
    block = (rows, width)
    return pl.pallas_call(
        kernel,
        out_shape=jax.ShapeDtypeStruct(block, jnp.bfloat16),
        in_specs=[hbm] * 6,
        out_specs=vmem,
        scratch_shapes=[
            pltpu.VMEM(routes.shape[::-1], routes.dtype),
            pltpu.VMEM(router_weight.shape[::-1], router_weight.dtype),
            pltpu.VMEM((4, 4) + block, jnp.bfloat16),
            pltpu.VMEM((4, width, 2 * hidden_units), jnp.bfloat16),
            pltpu.VMEM((4, hidden_units, width), jnp.bfloat16),
            pltpu.VMEM((4, 2) + block, jnp.float32),
            pltpu.VMEM((4, 2) + block, jnp.bfloat16),
            pltpu.VMEM((4, 2) + block, jnp.bfloat16),
            pltpu.VMEM((4,) + block, jnp.bfloat16),
            pltpu.VMEM((4,) + block, jnp.bfloat16),
            pltpu.VMEM((4,) + block, jnp.bfloat16),
            pltpu.VMEM((4,) + block, jnp.bfloat16),
            pltpu.SemaphoreType.DMA((15,)),
            pltpu.SemaphoreType.DMA((23 * PIECES + 4,)),
            pltpu.SemaphoreType.DMA((23 * PIECES + 4,)),
        ],
        compiler_params=pltpu.CompilerParams(
            collective_id=0, has_side_effects=True, vmem_limit_bytes=60 * 2**20
        ),
    )(tokens, routes.T, router_weight.T, gate_weight, up_weight, down_weight)


def solution(mesh):
    def local(*args):
        tokens, routes, router_weight = args[:3]
        rows, top = routes.shape
        experts = router_weight.shape[1]
        sec, sub = mesh.shape["sec"], mesh.shape["sub"]
        if experts == sec == sub == 4 and 2 * rows * top // experts >= rows and rows % 16 == 0:
            return dense(*args)
        return routed(*args)

    placed = (
        P(("group", "sec"), "sub"),
        P(("group", "sec"), None),
        P(),
        P("sec", None, "sub"),
        P("sec", None, "sub"),
        P("sec", "sub", None),
    )
    return jax.shard_map(
        local, mesh=mesh, in_specs=placed, out_specs=P(("group", "sec"), "sub"), check_vma=False
    )
```

```python
import functools
import jax
import jax.numpy as jnp
from jax import lax
from jax.experimental import pallas as pl
from jax.experimental.pallas import tpu as pltpu
from jax.sharding import PartitionSpec as P


def routed(tokens, routes, router_weight, gate_weight, up_weight, down_weight):
    rows, top = routes.shape
    experts = router_weight.shape[1]
    slots = 2 * rows * top // experts
    flat_ids = routes.reshape(-1)
    onehot = (flat_ids[:, None] == jnp.arange(experts, dtype=jnp.int32)[None, :]).astype(jnp.int32)
    before = jnp.cumsum(onehot, axis=0) - onehot
    position = jnp.sum(before * onehot, axis=1)
    target = flat_ids * slots + position
    placing = target[None, :] == jnp.arange(experts * slots, dtype=jnp.int32)[:, None]
    dispatch = jnp.sum(
        placing.reshape(experts * slots, rows, top).astype(jnp.int32), axis=2
    ).astype(jnp.bfloat16)
    full_rows = lax.all_gather(tokens, "sub", axis=1, tiled=True)
    logits = jnp.dot(full_rows, router_weight, preferred_element_type=jnp.float32)
    outgoing = jnp.dot(dispatch, full_rows, preferred_element_type=jnp.float32).astype(jnp.bfloat16)
    arrived = lax.all_to_all(
        outgoing.reshape(experts, slots, -1), "sec", split_axis=0, concat_axis=0, tiled=True
    )
    arrived = arrived.reshape(experts * slots, -1)
    chosen = jnp.sum(
        onehot.reshape(rows, top, experts).astype(jnp.float32) * logits[:, None, :], axis=2
    )
    raised = jnp.exp(chosen)
    gates = (raised / jnp.sum(raised, axis=1, keepdims=True)).astype(jnp.bfloat16)
    weighted = jnp.where(placing, gates.reshape(-1)[None, :], jnp.zeros((), jnp.bfloat16))
    combine = jnp.sum(
        weighted.reshape(experts * slots, rows, top).astype(jnp.float32), axis=2
    ).astype(jnp.bfloat16)
    gate_part = jnp.dot(arrived, gate_weight[0], preferred_element_type=jnp.float32)
    up_part = jnp.dot(arrived, up_weight[0], preferred_element_type=jnp.float32)
    hidden = (jax.nn.silu(gate_part) * up_part).astype(jnp.bfloat16)
    partial_value = jnp.dot(hidden, down_weight[0], preferred_element_type=jnp.float32).astype(
        jnp.bfloat16
    )
    contract = (((0,), (0,)), ((), ()))
    returned = lax.all_to_all(
        partial_value.reshape(experts, slots, -1), "sec", split_axis=0, concat_axis=0, tiled=True
    )
    returned = returned.reshape(experts * slots, -1)
    combined = lax.dot_general(combine, returned, contract, preferred_element_type=jnp.float32)
    mixed = lax.psum_scatter(combined.astype(jnp.bfloat16), "sub", scatter_dimension=1, tiled=True)
    return mixed


PIECES = 2


def flip(index, step):
    if step == 0:
        return index
    if step == 1:
        return index + 1 - 2 * (index % 2)
    if step == 2:
        return (index + 2) % 4
    return 3 - index


def kernel(
    tokens, routes_hbm, router_hbm, gate_w, up_w, down_w, out,
    routes, router, x, wide, down, keep, core_out, core_in, side_out, side_in, far_out, far_in,
    load_sem, send_sem, recv_sem,
):
    group, sec, sub = (lax.axis_index(name) for name in ("group", "sec", "sub"))
    width = tokens.shape[1]
    hidden_units = gate_w.shape[2]
    rows, top = tokens.shape[0], routes.shape[0]
    experts = router.shape[0]

    loads = [pltpu.make_async_copy(tokens, x.at[0, 0], load_sem.at[0])]
    for j in range(4):
        part = pl.ds(pl.multiple_of(flip(sub, j) * width, width), width)
        loads.append(
            pltpu.make_async_copy(
                gate_w.at[0, part, :], wide.at[j, :, pl.ds(0, hidden_units)], load_sem.at[1 + j]
            )
        )
        loads.append(
            pltpu.make_async_copy(
                up_w.at[0, part, :], wide.at[j, :, pl.ds(hidden_units, hidden_units)],
                load_sem.at[5 + j],
            )
        )
    for j in range(4):
        part = pl.ds(pl.multiple_of(flip(sub, j) * width, width), width)
        loads.append(pltpu.make_async_copy(down_w.at[0, :, part], down.at[j], load_sem.at[9 + j]))
    loads.append(pltpu.make_async_copy(routes_hbm, routes, load_sem.at[13]))
    loads.append(pltpu.make_async_copy(router_hbm, router, load_sem.at[14]))
    barrier = pltpu.get_barrier_semaphore()
    partners = [(group, flip(sec, k), sub) for k in (1, 2, 3)]
    partners = partners[::-1] + [(group, sec, flip(sub, j)) for j in (2, 1)]
    for partner in partners:
        pl.semaphore_signal(
            barrier, inc=1, device_id=partner, device_id_type=pl.DeviceIdType.MESH
        )
    for load in loads:
        load.start()
    pl.semaphore_wait(barrier, len(partners))

    used = [0]

    def copy(source, target, over_sec, over_sub, landing=None):
        number = used[0]
        used[0] += 1
        return pltpu.make_async_remote_copy(
            src_ref=source,
            dst_ref=target,
            send_sem=send_sem.at[number],
            recv_sem=recv_sem.at[number if landing is None else landing],
            device_id=(group, flip(sec, over_sec), flip(sub, over_sub)),
            device_id_type=pl.DeviceIdType.MESH,
        )

    cuts = [pl.ds(h * (rows // PIECES), rows // PIECES) for h in range(PIECES)]

    def copies(source, target, over_sec, over_sub):
        return [copy(source.at[cut], target.at[cut], over_sec, over_sub) for cut in cuts]

    gather_far = {k: copies(x.at[0, 0], x.at[k, 0], k, 0) for k in (1, 2, 3)}
    gather_far["twin"] = copies(x.at[0, 2], x.at[1, 2], 1, 0)
    relay = [
        copy(x.at[2, 0].at[cut], x.at[3, 0].at[cut], 1, 0, 2 * PIECES + h)
        for h, cut in enumerate(cuts)
    ]
    gather_core = {k: copies(x.at[k, 0], x.at[k, 1], 0, 1) for k in range(4)}
    gather_side = {k: copies(x.at[k, 0], x.at[k, 2], 0, 2) for k in (0, 2, 3)}
    gather_last = {k: copies(x.at[k, 2], x.at[k, 3], 0, 1) for k in range(4)}
    sum_core = {k: copy(core_out.at[k], core_in.at[k], 0, 1) for k in range(4)}
    sum_side = {k: copies(side_out.at[k], side_in.at[k], 0, 2) for k in (0, 2, 3)}
    sum_far = {k: copies(far_out.at[k], far_in.at[k], k, 0) for k in (1, 2, 3)}
    sum_far["twin"] = copies(far_out.at[0], far_in.at[0], 1, 0)
    every = range(PIECES)

    def pass_on(k, h):
        gather_far[k][h].wait_recv()
        if k == 2:

            @pl.when(inner)
            def _():
                relay[h].start()

        if k != 1:
            gather_side[k][h].start()
        gather_core[k][h].start()

    def pass_last(k, h):
        (gather_far["twin"] if k == 1 else gather_side[k])[h].wait_recv()
        gather_last[k][h].start()

    def expert(k):
        for h in every:
            gather_core[k][h].wait_recv()
            gather_last[k][h].wait_recv()
        both = jnp.dot(x[k, 0], wide[0], preferred_element_type=jnp.float32)
        for j in (1, 2, 3):
            both += jnp.dot(x[k, j], wide[j], preferred_element_type=jnp.float32)
        hidden = (jax.nn.silu(both[:, :hidden_units]) * both[:, hidden_units:]).astype(jnp.bfloat16)
        if k == 0:
            for load in loads[9:13]:
                load.wait()
        for place, j in enumerate((1, 3)):
            core_out[k, place] = jnp.dot(
                hidden, down[j], preferred_element_type=jnp.float32
            ).astype(jnp.bfloat16)
        sum_core[k].start()
        for place, j in enumerate((0, 2)):
            keep[k, place] = jnp.dot(hidden, down[j], preferred_element_type=jnp.float32)

    def to_side(k):
        sum_core[k].wait_recv()
        for h in every:
            side_out[k, cuts[h]] = (
                keep[k, 1, cuts[h]] + core_in[k, 1, cuts[h]].astype(jnp.float32)
            ).astype(jnp.bfloat16)
            sum_side[k][h].start()

    def to_far(k, h):
        sum_side[k][h].wait_recv()
        far_out[k, cuts[h]] = (
            keep[k, 0, cuts[h]]
            + core_in[k, 0, cuts[h]].astype(jnp.float32)
            + side_in[k, cuts[h]].astype(jnp.float32)
        ).astype(jnp.bfloat16)
        sum_far[k][h].start()

    def both_to_next():
        sum_core[1].wait_recv()
        for place, slot, name in ((1, 0, "twin"), (0, 1, 1)):
            for h in every:
                far_out[slot, cuts[h]] = (
                    keep[1, place, cuts[h]] + core_in[1, place, cuts[h]].astype(jnp.float32)
                ).astype(jnp.bfloat16)
                sum_far[name][h].start()

    def gates():
        loads[13].wait()
        loads[14].wait()
        logits = jnp.zeros((experts, rows), jnp.float32)
        for j in range(4):
            part = pl.ds(pl.multiple_of(flip(sub, j) * width, width), width)
            logits += lax.dot_general(
                router[:, part], x[0, j], (((1,), (1,)), ((), ())),
                preferred_element_type=jnp.float32,
            )
        names = [routes[t : t + 1, :] for t in range(top)]
        raised = []
        for t in range(top):
            chosen = jnp.zeros((1, rows), jnp.float32)
            for e in range(experts):
                chosen = jnp.where(names[t] == e, logits[e : e + 1, :], chosen)
            raised.append(jnp.exp(chosen))
        whole = sum(raised)
        shares = [(r / whole).astype(jnp.bfloat16).astype(jnp.float32) for r in raised]
        lines = []
        for k in range(4):
            line = jnp.zeros((1, rows), jnp.float32)
            for t in range(top):
                line += jnp.where(names[t] == flip(sec, k), shares[t], 0.0)
            lines.append(line)
        lines.append(jnp.zeros((4, rows), jnp.float32))
        return jnp.transpose(jnp.concatenate(lines, axis=0))

    loads[0].wait()
    for h in every:
        gather_side[0][h].start()
        gather_far[2][h].start()
    for h in every:
        gather_core[0][h].start()
    for h in every:
        gather_far[1][h].start()
    inner = jnp.logical_or(sec == 1, sec == 2)

    @pl.when(inner)
    def _():
        for h in every:
            gather_far[3][h].start()

    for h in every:
        pass_last(0, h)
        gather_far["twin"][h].start()
    for h in every:
        pass_on(2, h)
    for h in every:
        pass_on(1, h)
    for load in loads[1:9]:
        load.wait()
    expert(0)
    for h in every:
        pass_on(3, h)
        pass_last(2, h)
        pass_last(1, h)
    expert(2)
    expert(1)
    to_side(2)
    for h in every:
        pass_last(3, h)
    both_to_next()
    expert(3)
    to_side(3)
    for h in every:
        to_far(2, h)
    weights = gates()
    sum_core[0].wait_recv()
    first, second = weights[:, 0:1], weights[:, 1:2]
    for h in every:
        sum_far["twin"][h].wait_recv()
    side_out[0] = (
        first * (keep[0, 1] + core_in[0, 1].astype(jnp.float32))
        + second * far_in[0].astype(jnp.float32)
    ).astype(jnp.bfloat16)
    for h in every:
        sum_side[0][h].start()
    for h in every:
        to_far(3, h)
    for h in every:
        sum_far[1][h].wait_recv()
    mixed = (
        first * (keep[0, 0] + core_in[0, 0].astype(jnp.float32))
        + second * far_in[1].astype(jnp.float32)
    )
    for h in every:
        sum_far[2][h].wait_recv()
    mixed += weights[:, 2:3] * far_in[2].astype(jnp.float32)
    for h in every:
        sum_side[0][h].wait_recv()
    mixed += side_in[0].astype(jnp.float32)
    for h in every:
        sum_far[3][h].wait_recv()
    out[...] = (mixed + weights[:, 3:4] * far_in[3].astype(jnp.float32)).astype(jnp.bfloat16)
    for family in (gather_far, gather_core, gather_side, gather_last, sum_side, sum_far):
        for name in family:
            if family is gather_far and name == 3:
                continue
            for h in every:
                family[name][h].wait_send()

    @pl.when(inner)
    def _():
        for h in every:
            gather_far[3][h].wait_send()
            relay[h].wait_send()

    for k in range(4):
        sum_core[k].wait_send()


def dense(tokens, routes, router_weight, gate_weight, up_weight, down_weight):
    rows, width = tokens.shape
    hidden_units = gate_weight.shape[2]
    hbm, vmem = pl.BlockSpec(memory_space=pltpu.HBM), pl.BlockSpec(memory_space=pltpu.VMEM)
    block = (rows, width)
    return pl.pallas_call(
        kernel,
        out_shape=jax.ShapeDtypeStruct(block, jnp.bfloat16),
        in_specs=[hbm] * 6,
        out_specs=vmem,
        scratch_shapes=[
            pltpu.VMEM(routes.shape[::-1], routes.dtype),
            pltpu.VMEM(router_weight.shape[::-1], router_weight.dtype),
            pltpu.VMEM((4, 4) + block, jnp.bfloat16),
            pltpu.VMEM((4, width, 2 * hidden_units), jnp.bfloat16),
            pltpu.VMEM((4, hidden_units, width), jnp.bfloat16),
            pltpu.VMEM((4, 2) + block, jnp.float32),
            pltpu.VMEM((4, 2) + block, jnp.bfloat16),
            pltpu.VMEM((4, 2) + block, jnp.bfloat16),
            pltpu.VMEM((4,) + block, jnp.bfloat16),
            pltpu.VMEM((4,) + block, jnp.bfloat16),
            pltpu.VMEM((4,) + block, jnp.bfloat16),
            pltpu.VMEM((4,) + block, jnp.bfloat16),
            pltpu.SemaphoreType.DMA((15,)),
            pltpu.SemaphoreType.DMA((23 * PIECES + 4,)),
            pltpu.SemaphoreType.DMA((23 * PIECES + 4,)),
        ],
        compiler_params=pltpu.CompilerParams(
            collective_id=0, has_side_effects=True, vmem_limit_bytes=60 * 2**20
        ),
    )(tokens, routes.T, router_weight.T, gate_weight, up_weight, down_weight)


def solution(mesh):
    def local(*args):
        tokens, routes, router_weight = args[:3]
        rows, top = routes.shape
        experts = router_weight.shape[1]
        sec, sub = mesh.shape["sec"], mesh.shape["sub"]
        if experts == sec == sub == 4 and 2 * rows * top // experts >= rows and rows % 16 == 0:
            return dense(*args)
        return routed(*args)

    placed = (
        P(("group", "sec"), "sub"),
        P(("group", "sec"), None),
        P(),
        P("sec", None, "sub"),
        P("sec", None, "sub"),
        P("sec", "sub", None),
    )
    return jax.shard_map(
        local, mesh=mesh, in_specs=placed, out_specs=P(("group", "sec"), "sub"), check_vma=False
    )
```
